32 devices in a mesh: dp: 2 (over x), tensor: 4 (over y, core), section: 4 (over z).
Axes of the slice: x: 2, y: 2, z: 4, core: 2. Of those that a mesh axis runs over, the one named last changes fastest.
Arguments:
- grads: bfloat16 [2, 8, 768, 768], P('dp', 'section', 'tensor'), may hold values from -3 to 3
- owner: int32 [8, 1], P('section'), may hold values from 0 to 1; in each aligned block of 2 rows (0 to 1, 2 to 3, ...) at most 2 rows name the same one
- left_stat: float32 [2, 4, 2, 768, 768], P('dp', 'section', None, 'tensor')
- right_stat: float32 [2, 4, 2, 768, 768], P('dp', 'section', None, 'tensor')
- second_moment: float32 [2, 4, 2, 768, 768], P('dp', 'section', None, 'tensor'), may hold values from 0.05 to 4.5
- left_root: bfloat16 [2, 4, 2, 768, 768], P('dp', 'section', None, 'tensor')
- right_root: bfloat16 [2, 4, 2, 768, 768], P('dp', 'section', None, 'tensor')
Outputs:
- left_new: float32 [2, 4, 2, 768, 768], P('dp', 'section', None, 'tensor')
- right_new: float32 [2, 4, 2, 768, 768], P('dp', 'section', None, 'tensor')
- second_new: float32 [2, 4, 2, 768, 768], P('dp', 'section', None, 'tensor')
- direction: bfloat16 [2, 4, 2, 768, 768], P('dp', 'section', None, 'tensor')
The draws below stay inside these ranges and needn't reach their ends.
Inputs may be any that keep to these rules, and one draw needn't show every extreme that they name: `owner`: among the 2 blocks of one section, no dp rank owns more than 2.
All inputs are finite; a program needn't handle non-finite values.
Results may differ from the reference program's by a relative error of at most 0.02.
Values may be sent and summed in bfloat16 or wider, within the bound.
A program may use at most 128 MiB of HBM per device.

```python
import math
import jax
import jax.numpy as jnp
import numpy as np
from jax import lax

WIDTH = 768
CAP = 2
BLK_ST = 2
NB = 8
N_DP = 2
N_TENSOR = 4
N_SECTION = 4


def block_factor(key, low, high):
    shape = (N_DP, N_SECTION, CAP, N_TENSOR)
    values = jnp.exp(jax.random.uniform(key, shape, jnp.float32, math.log(low), math.log(high)))
    return jnp.repeat(values, WIDTH // N_TENSOR, axis=-1)


def symmetric_block(key, diag_low, diag_high, off_scale, rising):
    shape = (N_DP, N_SECTION, CAP, WIDTH, WIDTH)
    first_key, second_key = jax.random.split(key)
    noise = jax.random.normal(first_key, shape, jnp.float32) * off_scale
    noise = (noise + jnp.swapaxes(noise, -1, -2)) * 0.70710678
    diag_vals = jnp.exp(jax.random.uniform(second_key, shape[:-1], jnp.float32, math.log(diag_low), math.log(diag_high)))
    if rising:
        diag_vals = diag_vals * block_factor(jax.random.fold_in(key, 21), 1.0, 3.0)
    on_diag = jnp.arange(WIDTH)[:, None] == jnp.arange(WIDTH)[None, :]
    return jnp.where(on_diag, diag_vals[..., :, None], noise)


def draw_left_stat(key, part):
    return symmetric_block(jax.random.fold_in(key, 11), 4.0, 40.0, 0.5, False)


def draw_right_stat(key, part):
    return symmetric_block(jax.random.fold_in(key, 12), 4.0, 40.0, 0.5, False)


def draw_left_root(key, part):
    return symmetric_block(jax.random.fold_in(key, 13), 0.25, 0.35, 0.01, True).astype(jnp.bfloat16)


def draw_right_root(key, part):
    return symmetric_block(jax.random.fold_in(key, 14), 0.25, 0.35, 0.01, True).astype(jnp.bfloat16)


def draw_second_moment(key, part):
    shape = (N_DP, N_SECTION, CAP, WIDTH, WIDTH)
    inner = jax.random.fold_in(key, 15)
    base = jnp.exp(jax.random.uniform(inner, shape, jnp.float32, math.log(0.05), math.log(0.5)))
    factor = block_factor(jax.random.fold_in(key, 16), 1.0, 9.0)
    return base * factor[..., :, None]


def spiked(values, own_key, source, target, shards_of, factor):
    owner, partner = [(jnp.arange(values.shape[dim]) // (values.shape[dim] // shards_of)).reshape([-1 if axis == dim else 1 for axis in range(values.ndim)]) for dim in (source, target)]
    chosen = jax.random.permutation(own_key, shards_of)[partner]
    strong = (owner == chosen) | (owner == (partner + shards_of // 2) % shards_of)
    return jnp.where(strong, factor * values, values)


def block_scale(own_key, extent, cuts, low, largest):
    loudness, own = 1.0, jax.random.fold_in(own_key, 6)
    for position, shards_of in cuts:
        heights = jnp.exp(jax.random.uniform(jax.random.fold_in(own, position), (shards_of,), jnp.float32, low / len(cuts), largest / len(cuts)))
        loudness = loudness * jnp.repeat(heights, extent[position] // shards_of).reshape([-1 if axis == position else 1 for axis in range(len(extent))])
    return loudness


def deal_out(stream_key, own, number, rows, count, top, limit, slope):
    sequence = jax.random.permutation(stream_key, count)
    heavy_load, ordinary = shares(count, rows * top, limit, slope, True), shares(count, rows * top, limit, slope, False)
    places = jnp.arange(count)

    def named(lengths, turn):
        used = int((lengths > 0).sum())
        fixed = max(1, used // 4)
        moved = fixed + (places - fixed + turn * (used - fixed)) % max(1, count - fixed)
        return jnp.zeros((count,), jnp.int32).at[sequence[jnp.where(places < fixed, places, moved)]].set(jnp.asarray(lengths, jnp.int32))

    lengths = jnp.where(number % 4 == 0, named(heavy_load, number // 4), named(ordinary, number - number // 4 - 1))
    mixed = jax.random.permutation(jax.random.fold_in(own, 3), count)
    giver, receiver = mixed[0:count // 2 * 2:2], mixed[1:count // 2 * 2:2]
    margin = jnp.minimum(lengths[giver] - 1, limit - lengths[receiver]) // 2
    margin = jnp.where((giver == sequence[0]) | (receiver == sequence[0]) | (lengths[receiver] == 0), 0, jnp.maximum(margin, 0))
    moved = jax.random.randint(jax.random.fold_in(own, 4), (count // 2,), 0, 1 << 20) % (margin + 1)
    lengths = lengths.at[giver].add(-moved).at[receiver].add(moved)
    items = jnp.searchsorted(jnp.cumsum(lengths), jnp.arange(rows * top), side="right").astype(jnp.int32)
    table = items.reshape(top, rows).T
    table = table[jax.random.permutation(jax.random.fold_in(own, 1), rows)]
    turn = jax.random.randint(jax.random.fold_in(own, 2), (rows, 1), 0, top)
    return jnp.take_along_axis(table, (jnp.arange(top)[None, :] + turn) % top, axis=1)


def shares(count, total, bound, skew, full):
    portions = [(1 << 20) // math.isqrt(grade ** skew) + 1 for grade in range(1, count + 1)]
    largest = bound if full else min(bound, max(-(-total // count), total * portions[0] // sum(portions)))
    least = 1 if total - largest >= count - 1 else 0
    holding, surplus = [largest] + [least] * (count - 1), total - largest - least * (count - 1)
    while surplus > 0:
        free = [i for i in range(1, count) if holding[i] < largest] or [i for i in range(1, count) if holding[i] < bound]
        whole, budget = sum([portions[i] for i in free]), surplus
        for i in free:
            addition = min(bound - holding[i], max(1, budget * portions[i] // whole), surplus)
            holding[i] = holding[i] + addition
            surplus = surplus - addition
    return np.array(holding)


def gaussian_with(rng, extent, width, reach, pieces, heavy, held_as=jnp.bfloat16):
    result = width * jax.random.normal(rng, extent, jnp.float32)
    if pieces:
        result = result * block_scale(rng, extent, pieces, -0.22, 0.18)
    return jnp.clip(spiked(result, jax.random.fold_in(rng, 3), *heavy), -reach, reach).astype(held_as)


def setup_inputs(seed: int = 0) -> dict:
    key_of = jax.random.split(jax.random.key(seed), 8)
    grads = gaussian_with(key_of[0], (N_DP, NB, WIDTH, WIDTH), (0.5 / N_DP ** 0.5), 3.0, ((0, 2), (1, 4), (2, 4)), (0, 1, 2, 2.0))
    owner_keys = jax.random.split(jax.random.fold_in(key_of[1], 1), NB // BLK_ST)
    owner_turns = jax.random.permutation(jax.random.fold_in(key_of[1], 3), NB // BLK_ST)
    owner = jax.vmap(lambda own, number: deal_out(jax.random.fold_in(key_of[1], 2), own, number, BLK_ST, N_DP, 1, CAP, 2))(owner_keys, owner_turns).reshape((NB, 1))
    left_stat = draw_left_stat(jax.random.fold_in(key_of[7], 71), 0)
    right_stat = draw_right_stat(jax.random.fold_in(key_of[7], 71), 0)
    second_moment = draw_second_moment(jax.random.fold_in(key_of[7], 71), 0)
    left_root = draw_left_root(jax.random.fold_in(key_of[7], 71), 0)
    right_root = draw_right_root(jax.random.fold_in(key_of[7], 71), 0)
    return {"grads": grads, "owner": owner, "left_stat": left_stat, "right_stat": right_stat, "second_moment": second_moment, "left_root": left_root, "right_root": right_root}


def slot_index(owner):
    owners_grid = owner[:, 0].reshape(N_SECTION, BLK_ST)
    positions = jnp.arange(BLK_ST, dtype=jnp.int32)
    same_owner = owners_grid[:, :, None] == owners_grid[:, None, :]
    earlier = positions[None, :] < positions[:, None]
    ranked = lax.optimization_barrier(jnp.sum((same_owner & earlier[None]).astype(jnp.int32), axis=2))
    ranks_dp = jnp.arange(N_DP, dtype=jnp.int32)
    slot_ids = jnp.arange(CAP, dtype=jnp.int32)
    chosen = (owners_grid[None, :, None, :] == ranks_dp[:, None, None, None]) & (ranked[None, :, None, :] == slot_ids[None, None, :, None])
    local_pos = lax.optimization_barrier(jnp.sum(chosen.astype(jnp.int32) * positions[None, None, None, :], axis=3))
    section_base = (jnp.arange(N_SECTION, dtype=jnp.int32) * BLK_ST)[None, :, None]
    return ((local_pos + section_base).astype(jnp.int32), jnp.any(chosen, axis=3))

def one_slot(inputs):
    gradient, left_stat, right_stat, second_moment, left_root, right_root = inputs
    grad_wide = gradient.astype(jnp.float32)
    left_new = 0.95 * left_stat + 0.05 * jnp.dot(gradient, gradient.T, preferred_element_type=jnp.float32)
    right_new = 0.95 * right_stat + 0.05 * jnp.dot(gradient.T, gradient, preferred_element_type=jnp.float32)
    second_new = 0.9 * second_moment + 0.1 * grad_wide * grad_wide
    adam_dir = grad_wide / (jnp.sqrt(second_new) + 1e-08)
    mixed = jnp.dot(left_root, gradient, preferred_element_type=jnp.float32).astype(jnp.bfloat16)
    precond = jnp.dot(mixed, right_root, preferred_element_type=jnp.float32)
    scaling = jnp.sqrt(jnp.sum(adam_dir * adam_dir)) / jnp.sqrt(jnp.sum(precond * precond) + 1e-06)
    direction = (precond * scaling).astype(jnp.bfloat16)
    return (left_new, right_new, second_new, direction)

def reference(grads, owner, left_stat, right_stat, second_moment, left_root, right_root):

    def accumulate(total, replica):
        return (total + replica.astype(jnp.float32), None)
    summed, unused = lax.scan(accumulate, jnp.zeros((NB, WIDTH, WIDTH), jnp.float32), grads)
    index_table, occupied = slot_index(owner)
    slot_sum = jnp.take(summed, index_table.reshape(-1), axis=0)
    slot_sum = slot_sum * occupied.reshape(-1)[:, None, None].astype(jnp.float32)
    gradient = slot_sum.astype(jnp.bfloat16)
    count = N_DP * N_SECTION * CAP
    flat = (gradient, left_stat.reshape(count, WIDTH, WIDTH), right_stat.reshape(count, WIDTH, WIDTH), second_moment.reshape(count, WIDTH, WIDTH), left_root.reshape(count, WIDTH, WIDTH), right_root.reshape(count, WIDTH, WIDTH))
    left_new, right_new, second_new, direction = lax.map(one_slot, flat)
    shape = (N_DP, N_SECTION, CAP, WIDTH, WIDTH)
    return (left_new.reshape(shape), right_new.reshape(shape), second_new.reshape(shape), direction.reshape(shape))
```

```python
import functools

import jax
import jax.numpy as jnp
from jax import lax
from jax.experimental import pallas as pl
from jax.experimental.pallas import tpu as pltpu
from jax.sharding import PartitionSpec as P

CAP = 2
MESH = pl.DeviceIdType.MESH

X1, X2, X3, Y1, Y2, B1, B2, B3, B4, B5, B6 = range(0, 22, 2)
Z = 22


def plain_step(grads, owner, left_stat, right_stat, second_moment, left_root, right_root):
    block_count = owner.shape[0]
    my_rank = lax.axis_index("dp")
    owners_list = owner[:, 0]
    positions = jnp.arange(block_count, dtype=jnp.int32)
    same_owner = owners_list[:, None] == owners_list[None, :]
    earlier = positions[None, :] < positions[:, None]
    ranked = jnp.sum((same_owner & earlier).astype(jnp.int32), axis=1)
    slot_ids = jnp.arange(CAP, dtype=jnp.int32)
    local_grads = grads[0]
    chosen = (owners_list[None, :] == my_rank) & (ranked[None, :] == slot_ids[:, None])
    index_table = jnp.sum(chosen.astype(jnp.int32) * positions[None, :], axis=1)
    occupied = jnp.any(chosen, axis=1).astype(jnp.float32)
    summed = lax.psum(local_grads.astype(jnp.float32).astype(jnp.bfloat16), "dp").astype(
        jnp.float32
    )
    slot_sum = jnp.take(summed, index_table, axis=0) * occupied[:, None, None]
    gradient = slot_sum.astype(jnp.bfloat16)
    gathered = lax.all_gather(gradient, "tensor", axis=1, tiled=True)
    left_incr = jnp.einsum("cik,cjk->cij", gradient, gathered, preferred_element_type=jnp.float32)
    left_new = 0.95 * left_stat[0, 0] + 0.05 * left_incr
    partials = jnp.einsum("cki,ckj->cij", gradient, gradient, preferred_element_type=jnp.float32)
    right_incr = lax.psum_scatter(
        partials.astype(jnp.bfloat16), "tensor", scatter_dimension=1, tiled=True
    ).astype(jnp.float32)
    right_new = 0.95 * right_stat[0, 0] + 0.05 * right_incr
    grad_wide = gradient.astype(jnp.float32)
    second_new = 0.9 * second_moment[0, 0] + 0.1 * grad_wide * grad_wide
    adam_dir = grad_wide / (jnp.sqrt(second_new) + 1e-08)
    mixed = jnp.einsum(
        "cik,ckj->cij", left_root[0, 0], gathered, preferred_element_type=jnp.float32
    ).astype(jnp.bfloat16)
    precond = jnp.einsum(
        "cik,ckj->cij",
        mixed,
        lax.all_gather(right_root[0, 0], "tensor", axis=1, tiled=True),
        preferred_element_type=jnp.float32,
    )
    precond_sq = jnp.sum(precond * precond, axis=(1, 2))
    adam_sq = jnp.sum(adam_dir * adam_dir, axis=(1, 2))
    precond_sq, adam_sq = lax.psum((precond_sq, adam_sq), "tensor")
    scaling = jnp.sqrt(adam_sq) / jnp.sqrt(precond_sq + 1e-06)
    direction = (precond * scaling[:, None, None]).astype(jnp.bfloat16)
    return (
        left_new[None, None],
        right_new[None, None],
        second_new[None, None],
        direction[None, None],
    )


def fold(values):
    rows, columns = values.shape
    total = jnp.sum(values.reshape(rows // 8, 8, columns), axis=0)
    total = sum(total[:, i : i + 128] for i in range(0, columns, 128))
    return jnp.sum(total, axis=0, keepdims=True)


def kernel(
    owner, grads, left_stat, right_stat, second, left_root, right_root,
    left_out, right_out, second_out, direction_out,
    mine, theirs, summed, gradient, root_all, root_left, left_buf, right_buf, second_buf,
    mixed, precond, direction, turned, norms, local_sem, out_sem, send_sem, recv_sem,
):
    d, t = lax.axis_index("dp"), lax.axis_index("tensor")
    blocks, rows, width = mine.shape
    half, tile = rows // 2, 256
    tiles = width // tile
    other = 1 - d
    sibling, across, far = t + 1 - 2 * (t % 2), (t + 2) % 4, 3 - t
    peer_x, peer_s, peer_y = {"dp": other}, {"tensor": sibling}, {"tensor": across}
    peer_f = {"tensor": far}

    def load(k, source, target):
        return pltpu.make_async_copy(source, target, local_sem.at[k])

    def place(rank, r):
        return pl.ds(pl.multiple_of(rank * rows + r * half, 16), half)

    def whole(rank):
        return pl.ds(pl.multiple_of(rank * rows, 16), rows)

    def send(k, source, target, device):
        return pltpu.make_async_remote_copy(
            src_ref=source, dst_ref=target, send_sem=send_sem.at[k], recv_sem=recv_sem.at[k],
            device_id=device, device_id_type=MESH,
        )

    def go(k, source, target, device):
        copy = send(k, source, target, device)
        copy.start()
        sent.append(copy)

    def arrived(k, target, device):
        send(k, target, target, device).wait_recv()

    sent = []
    norms[t] = jnp.zeros((8, 128), jnp.float32)
    loads = [
        load(0, grads, mine),
        load(1, right_root, root_all.at[:, whole(t)]),
        load(2, second, second_buf),
        load(3, left_root, root_left),
        load(4, left_stat, left_buf),
        load(5, right_stat, right_buf),
    ]
    for copy in loads:
        copy.start()

    barrier = pltpu.get_barrier_semaphore()
    for peer in (peer_x, peer_s, peer_y, peer_f):
        pl.semaphore_signal(barrier, inc=1, device_id=peer, device_id_type=MESH)
    pl.semaphore_wait(barrier, 4)

    for r in range(2):
        part = pl.ds(r * half, half)
        go(X1 + r, grads.at[other, part], theirs.at[other, part], peer_x)
    go(Y2, right_root.at[0], root_all.at[0, whole(t)], peer_y)
    for r in range(2):
        part = pl.ds(r * half, half)
        go(X2 + r, grads.at[d, part], theirs.at[d, part], peer_x)
    for c in range(2):
        go(B5 + c, right_root.at[c], root_all.at[c, whole(t)], peer_s)

    def add(block, r):
        def body(i, carry):
            at = pl.ds(pl.multiple_of(r * half + i * 16, 16), 16)
            to = pl.ds(pl.multiple_of(t * rows + r * half + i * 16, 16), 16)
            total = mine[block, at].astype(jnp.float32) + theirs[block, at].astype(jnp.float32)
            summed[block, to] = total.astype(jnp.bfloat16)
            return carry

        lax.fori_loop(0, half // 16, body, 0, unroll=2)

    owners = [owner[b, 0] for b in range(blocks)]
    weights = []
    for c in range(CAP):
        row = []
        for b in range(blocks):
            if b < c:
                row.append(None)
                continue
            rank = sum(((owners[e] == owners[b]).astype(jnp.int32) for e in range(b)), jnp.int32(0))
            row.append(((owners[b] == d) & (rank == c)).astype(jnp.float32))
        weights.append(row)

    def select(first, count):
        def body(i, carry):
            at = pl.ds(pl.multiple_of(first + i * 16, 16), 16)
            terms = [summed[b, at].astype(jnp.float32) for b in range(blocks)]
            for c in range(CAP):
                total = sum(terms[b] * weights[c][b] for b in range(c, blocks))
                gradient[c, at] = total.astype(jnp.bfloat16)
            return carry

        lax.fori_loop(0, count // 16, body, 0, unroll=2)

    loads[0].wait()
    for r in range(2):
        arrived(X1 + r, theirs.at[d, pl.ds(r * half, half)], peer_x)
        add(d, r)
        go(Y1 + r, summed.at[d, place(t, r)], summed.at[d, place(t, r)], peer_y)
        go(B1 + r, summed.at[d, place(t, r)], summed.at[d, place(t, r)], peer_s)
    go(Y2 + 1, right_root.at[1], root_all.at[1, whole(t)], peer_y)
    for r in range(2):
        arrived(X2 + r, theirs.at[other, pl.ds(r * half, half)], peer_x)
        add(other, r)
        go(B2 + r, summed.at[other, place(t, r)], summed.at[other, place(t, r)], peer_s)
        arrived(Y1 + r, summed.at[d, place(across, r)], peer_y)
        go(X3 + r, summed.at[d, place(across, r)], summed.at[d, place(across, r)], peer_x)
        go(B3 + r, summed.at[d, place(across, r)], summed.at[d, place(across, r)], peer_s)
    arrived(Y2, root_all.at[0, whole(across)], peer_y)
    go(B6, root_all.at[0, whole(across)], root_all.at[0, whole(across)], peer_s)

    select(t * rows, rows)
    loads[2].wait()
    for c in range(CAP):

        def moment(i, total):
            at = pl.ds(pl.multiple_of(i * 16, 16), 16)
            g = gradient[c, pl.ds(pl.multiple_of(t * rows + i * 16, 16), 16)].astype(jnp.float32)
            new = 0.9 * second_buf[c, at] + 0.1 * g * g
            second_buf[c, at] = new
            adam = g / (jnp.sqrt(new) + 1e-08)
            return total + fold(adam * adam)

        norms[t, c : c + 1] = lax.fori_loop(
            0, rows // 16, moment, jnp.zeros((1, 128), jnp.float32)
        )
    stores = [pltpu.make_async_copy(second_buf, second_out, out_sem.at[0])]
    stores[0].start()

    for r in range(2):
        arrived(B1 + r, summed.at[d, place(sibling, r)], peer_s)
        arrived(B2 + r, summed.at[other, place(sibling, r)], peer_s)
    select(sibling * rows, rows)
    for r in range(2):
        arrived(X3 + r, summed.at[other, place(across, r)], peer_x)
        go(B4 + r, summed.at[other, place(across, r)], summed.at[other, place(across, r)], peer_s)
        select(across * rows + r * half, half)
    arrived(Y2 + 1, root_all.at[1, whole(across)], peer_y)
    go(B6 + 1, root_all.at[1, whole(across)], root_all.at[1, whole(across)], peer_s)
    for r in range(2):
        arrived(B3 + r, summed.at[d, place(far, r)], peer_s)
        arrived(B4 + r, summed.at[other, place(far, r)], peer_s)
        select(far * rows + r * half, half)
    loads[3].wait()

    def tiled(body):
        def step(i, carry):
            body(i // tiles, pl.ds(pl.multiple_of((i % tiles) * tile, tile), tile))
            return carry

        lax.fori_loop(0, CAP * tiles, step, 0)

    def mix(c, cut):
        mixed[c, :, cut] = jnp.dot(
            root_left[c], gradient[c, :, cut], preferred_element_type=jnp.float32
        ).astype(jnp.bfloat16)

    tiled(mix)
    loads[1].wait()
    for c in range(2):
        arrived(B5 + c, root_all.at[c, whole(sibling)], peer_s)
        arrived(B6 + c, root_all.at[c, whole(far)], peer_s)
    for c in range(CAP):

        def multiply(i, total):
            cut = pl.ds(pl.multiple_of(i * tile, tile), tile)
            product = jnp.dot(mixed[c], root_all[c, :, cut], preferred_element_type=jnp.float32)
            precond[c, :, cut] = product
            return total + fold(product * product)

        norms[t, CAP + c : CAP + c + 1] = lax.fori_loop(
            0, tiles, multiply, jnp.zeros((1, 128), jnp.float32)
        )
    for k, peer in enumerate((peer_s, peer_y, peer_f)):
        go(Z + k, norms.at[t], norms.at[t], peer)

    loads[4].wait()

    def left(c, cut):
        product = lax.dot_general(
            gradient[c, whole(t)], gradient[c, cut], (((1,), (1,)), ((), ())),
            preferred_element_type=jnp.float32,
        )
        left_buf[c, :, cut] = 0.95 * left_buf[c, :, cut] + 0.05 * product

    tiled(left)
    stores.append(pltpu.make_async_copy(left_buf, left_out, out_sem.at[1]))
    stores[1].start()
    loads[5].wait()
    window = pl.ds(pl.multiple_of(128 * ((3 * t) // 2), 128), tile)
    shift = pl.ds(pl.multiple_of(64 * (t % 2), 64), rows)
    for c in range(CAP):
        turned[c] = gradient[c, :, window].T

    def right(c, cut):
        product = jnp.dot(
            turned[c, shift], gradient[c, :, cut], preferred_element_type=jnp.float32
        )
        right_buf[c, :, cut] = 0.95 * right_buf[c, :, cut] + 0.05 * product

    tiled(right)
    stores.append(pltpu.make_async_copy(right_buf, right_out, out_sem.at[2]))
    stores[2].start()

    for k, (rank, peer) in enumerate(((sibling, peer_s), (across, peer_y), (far, peer_f))):
        arrived(Z + k, norms.at[rank], peer)
    total = jnp.sum(norms[0] + norms[1] + norms[2] + norms[3], axis=1, keepdims=True)
    for c in range(CAP):
        scaling = jnp.sqrt(total[c : c + 1]) / jnp.sqrt(total[CAP + c : CAP + c + 1] + 1e-06)

        def scale(i, carry):
            at = pl.ds(pl.multiple_of(i * 16, 16), 16)
            direction[c, at] = (precond[c, at] * scaling).astype(jnp.bfloat16)
            return carry

        lax.fori_loop(0, rows // 16, scale, 0, unroll=2)
    stores.append(pltpu.make_async_copy(direction, direction_out, out_sem.at[3]))
    stores[3].start()
    for copy in sent:
        copy.wait_send()
    for copy in stores:
        copy.wait()


def fused_step(grads, owner, left_stat, right_stat, second_moment, left_root, right_root):
    _, blocks, rows, width = grads.shape
    full = (CAP, width, width)
    part = (CAP, rows, width)
    f32, bf16 = jnp.float32, jnp.bfloat16
    anywhere = pl.BlockSpec(memory_space=pl.ANY)
    outs = pl.pallas_call(
        kernel,
        out_shape=[jax.ShapeDtypeStruct(part, f32)] * 3 + [jax.ShapeDtypeStruct(part, bf16)],
        in_specs=[pl.BlockSpec(memory_space=pltpu.SMEM)] + [anywhere] * 6,
        out_specs=[anywhere] * 4,
        scratch_shapes=[
            pltpu.VMEM((blocks, rows, width), bf16),
            pltpu.VMEM((blocks, rows, width), bf16),
            pltpu.VMEM((blocks, width, width), bf16),
            pltpu.VMEM(full, bf16),
            pltpu.VMEM(full, bf16),
            pltpu.VMEM(part, bf16),
            pltpu.VMEM(part, f32),
            pltpu.VMEM(part, f32),
            pltpu.VMEM(part, f32),
            pltpu.VMEM(part, bf16),
            pltpu.VMEM(part, f32),
            pltpu.VMEM(part, bf16),
            pltpu.VMEM((CAP, 256, width), bf16),
            pltpu.VMEM((4, 8, 128), f32),
            pltpu.SemaphoreType.DMA((6,)),
            pltpu.SemaphoreType.DMA((4,)),
            pltpu.SemaphoreType.DMA((Z + 3,)),
            pltpu.SemaphoreType.DMA((Z + 3,)),
        ],
        compiler_params=pltpu.CompilerParams(
            collective_id=0, has_side_effects=True, vmem_limit_bytes=48 * 1024 * 1024
        ),
    )(
        owner, grads[0], left_stat[0, 0], right_stat[0, 0], second_moment[0, 0],
        left_root[0, 0], right_root[0, 0],
    )
    return tuple(out[None, None] for out in outs)


def solution(mesh):
    state = P("dp", "section", None, "tensor", None)
    placed = (P("dp", "section", "tensor", None), P("section", None)) + (state,) * 5

    def step(*args):
        _, blocks, rows, width = args[0].shape
        fits = mesh.shape["dp"] == 2 and mesh.shape["tensor"] == 4 and blocks == 2
        fits = fits and rows == 192 and width == 768 and args[2].shape[2] == CAP
        return (fused_step if fits else plain_step)(*args)

    return jax.shard_map(
        step, mesh=mesh, in_specs=placed, out_specs=(state,) * 4, check_vma=False
    )
```

```python
import functools

import jax
import jax.numpy as jnp
from jax import lax
from jax.experimental import pallas as pl
from jax.experimental.pallas import tpu as pltpu
from jax.sharding import PartitionSpec as P

CAP = 2
MESH = pl.DeviceIdType.MESH

CHUNKS = 4
X1, X2, X3, Y1, Y2, B1, B2, B3, B4, B5, B6, Z = range(0, 12 * CHUNKS, CHUNKS)


def plain_step(grads, owner, left_stat, right_stat, second_moment, left_root, right_root):
    block_count = owner.shape[0]
    my_rank = lax.axis_index("dp")
    owners_list = owner[:, 0]
    positions = jnp.arange(block_count, dtype=jnp.int32)
    same_owner = owners_list[:, None] == owners_list[None, :]
    earlier = positions[None, :] < positions[:, None]
    ranked = jnp.sum((same_owner & earlier).astype(jnp.int32), axis=1)
    slot_ids = jnp.arange(CAP, dtype=jnp.int32)
    local_grads = grads[0]
    chosen = (owners_list[None, :] == my_rank) & (ranked[None, :] == slot_ids[:, None])
    index_table = jnp.sum(chosen.astype(jnp.int32) * positions[None, :], axis=1)
    occupied = jnp.any(chosen, axis=1).astype(jnp.float32)
    summed = lax.psum(local_grads.astype(jnp.float32).astype(jnp.bfloat16), "dp").astype(
        jnp.float32
    )
    slot_sum = jnp.take(summed, index_table, axis=0) * occupied[:, None, None]
    gradient = slot_sum.astype(jnp.bfloat16)
    gathered = lax.all_gather(gradient, "tensor", axis=1, tiled=True)
    left_incr = jnp.einsum("cik,cjk->cij", gradient, gathered, preferred_element_type=jnp.float32)
    left_new = 0.95 * left_stat[0, 0] + 0.05 * left_incr
    partials = jnp.einsum("cki,ckj->cij", gradient, gradient, preferred_element_type=jnp.float32)
    right_incr = lax.psum_scatter(
        partials.astype(jnp.bfloat16), "tensor", scatter_dimension=1, tiled=True
    ).astype(jnp.float32)
    right_new = 0.95 * right_stat[0, 0] + 0.05 * right_incr
    grad_wide = gradient.astype(jnp.float32)
    second_new = 0.9 * second_moment[0, 0] + 0.1 * grad_wide * grad_wide
    adam_dir = grad_wide / (jnp.sqrt(second_new) + 1e-08)
    mixed = jnp.einsum(
        "cik,ckj->cij", left_root[0, 0], gathered, preferred_element_type=jnp.float32
    ).astype(jnp.bfloat16)
    precond = jnp.einsum(
        "cik,ckj->cij",
        mixed,
        lax.all_gather(right_root[0, 0], "tensor", axis=1, tiled=True),
        preferred_element_type=jnp.float32,
    )
    precond_sq = jnp.sum(precond * precond, axis=(1, 2))
    adam_sq = jnp.sum(adam_dir * adam_dir, axis=(1, 2))
    precond_sq, adam_sq = lax.psum((precond_sq, adam_sq), "tensor")
    scaling = jnp.sqrt(adam_sq) / jnp.sqrt(precond_sq + 1e-06)
    direction = (precond * scaling[:, None, None]).astype(jnp.bfloat16)
    return (
        left_new[None, None],
        right_new[None, None],
        second_new[None, None],
        direction[None, None],
    )


def fold(values):
    rows, columns = values.shape
    total = jnp.sum(values.reshape(rows // 8, 8, columns), axis=0)
    total = sum(total[:, i : i + 128] for i in range(0, columns, 128))
    return jnp.sum(total, axis=0, keepdims=True)


def kernel(
    owner, grads, left_stat, right_stat, second, left_root, right_root,
    left_out, right_out, second_out, precond, totals,
    mine, theirs, summed, gradient, root_all, root_left,
    mixed, turned, norms, local_sem, send_sem, recv_sem,
):
    d, t = lax.axis_index("dp"), lax.axis_index("tensor")
    blocks, rows, width = mine.shape
    chunk, half, tile = rows // CHUNKS, rows // 2, 256
    tiles = width // tile
    other = 1 - d
    sibling, across, far = t + 1 - 2 * (t % 2), (t + 2) % 4, 3 - t
    peer_x, peer_s, peer_y = {"dp": other}, {"tensor": sibling}, {"tensor": across}
    peer_f = {"tensor": far}

    def load(k, source, target):
        return pltpu.make_async_copy(source, target, local_sem.at[k])

    def place(rank, r):
        return pl.ds(pl.multiple_of(rank * rows + r * chunk, 16), chunk)

    def whole(rank):
        return pl.ds(pl.multiple_of(rank * rows, 16), rows)

    def root_part(rank, k):
        return root_all.at[k // 2, pl.ds(pl.multiple_of(rank * rows + k % 2 * half, 16), half)]

    def send(k, source, target, device):
        return pltpu.make_async_remote_copy(
            src_ref=source, dst_ref=target, send_sem=send_sem.at[k], recv_sem=recv_sem.at[k],
            device_id=device, device_id_type=MESH,
        )

    def go(k, source, target, device):
        copy = send(k, source, target, device)
        copy.start()
        sent.append(copy)

    def arrived(k, target, device):
        send(k, target, target, device).wait_recv()

    def go_rows(k, block, at, device):
        go(k, summed.at[block, at], summed.at[block, at], device)

    def go_x(k):
        block, part = (other, d)[k // CHUNKS], pl.ds(k % CHUNKS * chunk, chunk)
        go(X1 + k, grads.at[block, part], theirs.at[block, part], peer_x)

    def go_root(k):
        source = right_root.at[k // 2, pl.ds(k % 2 * half, half)]
        go(Y2 + k, source, root_part(t, k), peer_y)

    def root_came(k):
        arrived(Y2 + k, root_part(across, k), peer_y)
        go(B6 + k, root_part(across, k), root_part(across, k), peer_s)

    sent = []
    norms[t] = jnp.zeros((8, 128), jnp.float32)
    loads = [
        load(0, grads, mine),
        load(1, right_root, root_all.at[:, whole(t)]),
        load(2, second, second_out),
        load(3, left_root, root_left),
        load(4, left_stat, left_out),
        load(5, right_stat, right_out),
    ]
    loads[0].start()

    barrier = pltpu.get_barrier_semaphore()
    for peer in (peer_x, peer_s, peer_y, peer_f):
        pl.semaphore_signal(barrier, inc=1, device_id=peer, device_id_type=MESH)
    pl.semaphore_wait(barrier, 4)

    go_x(0)
    go_root(0)
    go_x(1)
    for copy in loads[1:]:
        copy.start()
    for c in range(2):
        go(B5 + c, right_root.at[c], root_all.at[c, whole(t)], peer_s)

    def add(block, r):
        def body(i, carry):
            at = pl.ds(pl.multiple_of(r * chunk + i * 16, 16), 16)
            to = pl.ds(pl.multiple_of(t * rows + r * chunk + i * 16, 16), 16)
            total = mine[block, at].astype(jnp.float32) + theirs[block, at].astype(jnp.float32)
            summed[block, to] = total.astype(jnp.bfloat16)
            return carry

        lax.fori_loop(0, chunk // 16, body, 0)

    owners = [owner[b] for b in range(blocks)]
    weights = []
    for c in range(CAP):
        row = []
        for b in range(blocks):
            if b < c:
                row.append(None)
                continue
            rank = sum(((owners[e] == owners[b]).astype(jnp.int32) for e in range(b)), jnp.int32(0))
            row.append(((owners[b] == d) & (rank == c)).astype(jnp.float32))
        weights.append(row)

    def select(first, count):
        def body(i, carry):
            at = pl.ds(pl.multiple_of(first + i * 16, 16), 16)
            terms = [summed[b, at].astype(jnp.float32) for b in range(blocks)]
            for c in range(CAP):
                total = sum(terms[b] * weights[c][b] for b in range(c, blocks))
                gradient[c, at] = total.astype(jnp.bfloat16)
            return carry

        lax.fori_loop(0, count // 16, body, 0)

    def across_came(r):
        arrived(Y1 + r, summed.at[d, place(across, r)], peer_y)
        go_rows(X3 + r, d, place(across, r), peer_x)
        go_rows(B3 + r, d, place(across, r), peer_s)

    loads[0].wait()
    for r in range(CHUNKS):
        arrived(X1 + r, theirs.at[d, pl.ds(r * chunk, chunk)], peer_x)
        go_x(2 + r)
        add(d, r)
        go_rows(Y1 + r, d, place(t, r), peer_y)
        go_rows(B1 + r, d, place(t, r), peer_s)
        if r >= 2:
            across_came(r - 2)
    go_root(1)
    go_root(2)
    for r in range(CHUNKS):
        arrived(X2 + r, theirs.at[other, pl.ds(r * chunk, chunk)], peer_x)
        if 2 + CHUNKS + r < 2 * CHUNKS:
            go_x(2 + CHUNKS + r)
        add(other, r)
        go_rows(B2 + r, other, place(t, r), peer_s)
        if r + CHUNKS - 2 < CHUNKS:
            across_came(r + CHUNKS - 2)
    root_came(0)
    root_came(1)
    go_root(3)

    select(t * rows, rows)
    loads[2].wait()
    for c in range(CAP):

        def moment(i, total):
            at = pl.ds(pl.multiple_of(i * 16, 16), 16)
            g = gradient[c, pl.ds(pl.multiple_of(t * rows + i * 16, 16), 16)].astype(jnp.float32)
            new = 0.9 * second_out[c, at] + 0.1 * g * g
            second_out[c, at] = new
            adam = g / (jnp.sqrt(new) + 1e-08)
            return total + fold(adam * adam)

        norms[t, c : c + 1] = lax.fori_loop(
            0, rows // 16, moment, jnp.zeros((1, 128), jnp.float32)
        )

    for r in range(CHUNKS):
        arrived(X3 + r, summed.at[other, place(across, r)], peer_x)
        go_rows(B4 + r, other, place(across, r), peer_s)
        if r == 0:
            for k in range(CHUNKS):
                arrived(B1 + k, summed.at[d, place(sibling, k)], peer_s)
                arrived(B2 + k, summed.at[other, place(sibling, k)], peer_s)
            select(sibling * rows, rows)
        if r == 1:
            root_came(2)
        select(across * rows + r * chunk, chunk)
    root_came(3)
    for r in range(CHUNKS):
        arrived(B3 + r, summed.at[d, place(far, r)], peer_s)
        arrived(B4 + r, summed.at[other, place(far, r)], peer_s)
        select(far * rows + r * chunk, chunk)
    loads[3].wait()

    def tiled(body):
        def step(i, carry):
            body(i // tiles, pl.ds(pl.multiple_of((i % tiles) * tile, tile), tile))
            return carry

        lax.fori_loop(0, CAP * tiles, step, 0)

    def mix(c, cut):
        mixed[c, :, cut] = jnp.dot(
            root_left[c], gradient[c, :, cut], preferred_element_type=jnp.float32
        ).astype(jnp.bfloat16)

    tiled(mix)
    loads[1].wait()
    for c in range(2):
        arrived(B5 + c, root_all.at[c, whole(sibling)], peer_s)
    for k in range(4):
        arrived(B6 + k, root_part(far, k), peer_s)
    for c in range(CAP):

        def multiply(i, total):
            cut = pl.ds(pl.multiple_of(i * tile, tile), tile)
            product = jnp.dot(mixed[c], root_all[c, :, cut], preferred_element_type=jnp.float32)
            precond[c, :, cut] = product
            return total + fold(product * product)

        norms[t, CAP + c : CAP + c + 1] = lax.fori_loop(
            0, tiles, multiply, jnp.zeros((1, 128), jnp.float32)
        )
    for k, peer in enumerate((peer_s, peer_y, peer_f)):
        go(Z + k, norms.at[t], norms.at[t], peer)

    loads[4].wait()

    def left(c, cut):
        product = lax.dot_general(
            gradient[c, whole(t)], gradient[c, cut], (((1,), (1,)), ((), ())),
            preferred_element_type=jnp.float32,
        )
        left_out[c, :, cut] = 0.95 * left_out[c, :, cut] + 0.05 * product

    tiled(left)
    loads[5].wait()
    window = pl.ds(pl.multiple_of(128 * ((3 * t) // 2), 128), tile)
    shift = pl.ds(pl.multiple_of(64 * (t % 2), 64), rows)
    for c in range(CAP):
        turned[c] = gradient[c, :, window].T

    def right(c, cut):
        product = jnp.dot(
            turned[c, shift], gradient[c, :, cut], preferred_element_type=jnp.float32
        )
        right_out[c, :, cut] = 0.95 * right_out[c, :, cut] + 0.05 * product

    tiled(right)
    for copy in sent:
        copy.wait_send()
    for k, (rank, peer) in enumerate(((sibling, peer_s), (across, peer_y), (far, peer_f))):
        arrived(Z + k, norms.at[rank], peer)
    totals[...] = norms[0] + norms[1] + norms[2] + norms[3]


def finish(
    left, right, second, precond, totals,
    left_out, right_out, second_out, direction_out, direction, sems,
):
    rows = precond.shape[1]
    pairs = ((left, left_out), (right, right_out), (second, second_out))
    copies = [pltpu.make_async_copy(a, b, sems.at[k]) for k, (a, b) in enumerate(pairs)]
    for copy in copies:
        copy.start()
    total = jnp.sum(totals[...], axis=1, keepdims=True)
    for c in range(CAP):
        scaling = jnp.sqrt(total[c : c + 1]) / jnp.sqrt(total[CAP + c : CAP + c + 1] + 1e-06)

        def scale(i, carry):
            at = pl.ds(pl.multiple_of(i * 16, 16), 16)
            direction[c, at] = (precond[c, at] * scaling).astype(jnp.bfloat16)
            return carry

        lax.fori_loop(0, rows // 16, scale, 0, unroll=2)
        copies.append(
            pltpu.make_async_copy(direction.at[c], direction_out.at[c], sems.at[3 + c])
        )
        copies[-1].start()
    for copy in copies:
        copy.wait()


def fused_step(grads, owner, left_stat, right_stat, second_moment, left_root, right_root):
    _, blocks, rows, width = grads.shape
    full = (CAP, width, width)
    part = (CAP, rows, width)
    f32, bf16 = jnp.float32, jnp.bfloat16
    outside, inside = pl.BlockSpec(memory_space=pltpu.HBM), pl.BlockSpec(memory_space=pltpu.VMEM)
    big, small = jax.ShapeDtypeStruct(part, f32), jax.ShapeDtypeStruct((8, 128), f32)
    parts = pl.pallas_call(
        kernel,
        out_shape=[big] * 4 + [small],
        in_specs=[pl.BlockSpec(memory_space=pltpu.SMEM)] + [outside] * 6,
        out_specs=[inside] * 5,
        scratch_shapes=[
            pltpu.VMEM((blocks, rows, width), bf16),
            pltpu.VMEM((blocks, rows, width), bf16),
            pltpu.VMEM((blocks, width, width), bf16),
            pltpu.VMEM(full, bf16),
            pltpu.VMEM(full, bf16),
            pltpu.VMEM(part, bf16),
            pltpu.VMEM(part, bf16),
            pltpu.VMEM((CAP, 256, width), bf16),
            pltpu.VMEM((4, 8, 128), f32),
            pltpu.SemaphoreType.DMA((6,)),
            pltpu.SemaphoreType.DMA((Z + 3,)),
            pltpu.SemaphoreType.DMA((Z + 3,)),
        ],
        compiler_params=pltpu.CompilerParams(
            collective_id=0, has_side_effects=True, vmem_limit_bytes=32 * 1024 * 1024
        ),
    )(
        owner.reshape(blocks),
        *(
            pltpu.with_memory_space_constraint(x, pltpu.HBM)
            for x in (
                grads[0], left_stat[0, 0], right_stat[0, 0], second_moment[0, 0],
                left_root[0, 0], right_root[0, 0],
            )
        ),
    )
    outs = pl.pallas_call(
        finish,
        out_shape=[big] * 3 + [jax.ShapeDtypeStruct(part, bf16)],
        in_specs=[pl.BlockSpec(memory_space=pl.ANY)] * 3 + [inside] * 2,
        out_specs=[outside] * 4,
        scratch_shapes=[pltpu.VMEM(part, bf16), pltpu.SemaphoreType.DMA((3 + CAP,))],
        compiler_params=pltpu.CompilerParams(vmem_limit_bytes=16 * 1024 * 1024),
    )(*parts)
    return tuple(out[None, None] for out in outs)


def solution(mesh):
    state = P("dp", "section", None, "tensor", None)
    placed = (P("dp", "section", "tensor", None), P("section", None)) + (state,) * 5

    def step(*args):
        _, blocks, rows, width = args[0].shape
        fits = mesh.shape["dp"] == 2 and mesh.shape["tensor"] == 4 and blocks == 2
        fits = fits and rows == 192 and width == 768 and args[2].shape[2] == CAP
        return (fused_step if fits else plain_step)(*args)

    return jax.shard_map(
        step, mesh=mesh, in_specs=placed, out_specs=(state,) * 4, check_vma=False
    )
```

```python
import functools

import jax
import jax.numpy as jnp
from jax import lax
from jax.experimental import pallas as pl
from jax.experimental.pallas import tpu as pltpu
from jax.sharding import PartitionSpec as P

CAP = 2
MESH = pl.DeviceIdType.MESH

CHUNKS = 2
X1, X2, X3, Y1, Y2, B4, B6, B1, B2, B3, B5, Z = (*range(0, 14, 2), *range(14, 19))


def plain_step(grads, owner, left_stat, right_stat, second_moment, left_root, right_root):
    block_count = owner.shape[0]
    my_rank = lax.axis_index("dp")
    owners_list = owner[:, 0]
    positions = jnp.arange(block_count, dtype=jnp.int32)
    same_owner = owners_list[:, None] == owners_list[None, :]
    earlier = positions[None, :] < positions[:, None]
    ranked = jnp.sum((same_owner & earlier).astype(jnp.int32), axis=1)
    slot_ids = jnp.arange(CAP, dtype=jnp.int32)
    local_grads = grads[0]
    chosen = (owners_list[None, :] == my_rank) & (ranked[None, :] == slot_ids[:, None])
    index_table = jnp.sum(chosen.astype(jnp.int32) * positions[None, :], axis=1)
    occupied = jnp.any(chosen, axis=1).astype(jnp.float32)
    summed = lax.psum(local_grads.astype(jnp.float32).astype(jnp.bfloat16), "dp").astype(
        jnp.float32
    )
    slot_sum = jnp.take(summed, index_table, axis=0) * occupied[:, None, None]
    gradient = slot_sum.astype(jnp.bfloat16)
    gathered = lax.all_gather(gradient, "tensor", axis=1, tiled=True)
    left_incr = jnp.einsum("cik,cjk->cij", gradient, gathered, preferred_element_type=jnp.float32)
    left_new = 0.95 * left_stat[0, 0] + 0.05 * left_incr
    partials = jnp.einsum("cki,ckj->cij", gradient, gradient, preferred_element_type=jnp.float32)
    right_incr = lax.psum_scatter(
        partials.astype(jnp.bfloat16), "tensor", scatter_dimension=1, tiled=True
    ).astype(jnp.float32)
    right_new = 0.95 * right_stat[0, 0] + 0.05 * right_incr
    grad_wide = gradient.astype(jnp.float32)
    second_new = 0.9 * second_moment[0, 0] + 0.1 * grad_wide * grad_wide
    adam_dir = grad_wide / (jnp.sqrt(second_new) + 1e-08)
    mixed = jnp.einsum(
        "cik,ckj->cij", left_root[0, 0], gathered, preferred_element_type=jnp.float32
    ).astype(jnp.bfloat16)
    precond = jnp.einsum(
        "cik,ckj->cij",
        mixed,
        lax.all_gather(right_root[0, 0], "tensor", axis=1, tiled=True),
        preferred_element_type=jnp.float32,
    )
    precond_sq = jnp.sum(precond * precond, axis=(1, 2))
    adam_sq = jnp.sum(adam_dir * adam_dir, axis=(1, 2))
    precond_sq, adam_sq = lax.psum((precond_sq, adam_sq), "tensor")
    scaling = jnp.sqrt(adam_sq) / jnp.sqrt(precond_sq + 1e-06)
    direction = (precond * scaling[:, None, None]).astype(jnp.bfloat16)
    return (
        left_new[None, None],
        right_new[None, None],
        second_new[None, None],
        direction[None, None],
    )


def fold(values):
    rows, columns = values.shape
    total = jnp.sum(values.reshape(rows // 8, 8, columns), axis=0)
    return sum(total[:, i : i + 128] for i in range(0, columns, 128))


def kernel(
    owner, grads, left_stat, right_stat, second, left_root, right_root,
    left_out, right_out, second_out, precond, totals,
    mine, theirs, summed, gradient, root_all, root_left,
    mixed, turned, window_t, mixed_sum, right_sum, norms, local_sem, send_sem, recv_sem,
):
    d, t = lax.axis_index("dp"), lax.axis_index("tensor")
    blocks, rows, width = mine.shape
    chunk, half, tile = rows // CHUNKS, rows // 2, 256
    tiles = width // tile
    other = 1 - d
    sibling, across, far = t + 1 - 2 * (t % 2), (t + 2) % 4, 3 - t
    peer_x, peer_s, peer_y = {"dp": other}, {"tensor": sibling}, {"tensor": across}
    peer_f = {"tensor": far}

    def load(k, source, target):
        return pltpu.make_async_copy(source, target, local_sem.at[k])

    def place(rank, r):
        return pl.ds(pl.multiple_of(rank * rows + r * chunk, 16), chunk)

    def whole(rank):
        return pl.ds(pl.multiple_of(rank * rows, 16), rows)

    def root_part(rank, c):
        return root_all.at[c, whole(rank)]

    def send(k, source, target, device):
        return pltpu.make_async_remote_copy(
            src_ref=source, dst_ref=target, send_sem=send_sem.at[k], recv_sem=recv_sem.at[k],
            device_id=device, device_id_type=MESH,
        )

    def go(k, source, target, device):
        copy = send(k, source, target, device)
        copy.start()
        sent.append(copy)

    def arrived(k, target, device):
        send(k, target, target, device).wait_recv()

    def go_rows(k, block, at, device):
        go(k, summed.at[block, at], summed.at[block, at], device)

    def go_x(k):
        block, part = (other, d)[k // CHUNKS], pl.ds(k % CHUNKS * chunk, chunk)
        go(X1 + k, grads.at[block, part], theirs.at[block, part], peer_x)

    def go_root(c):
        go(Y2 + c, right_root.at[c], root_part(t, c), peer_y)

    def root_came(c):
        arrived(Y2 + c, root_part(across, c), peer_y)
        go(B6 + c, root_part(across, c), root_part(across, c), peer_s)

    sent = []
    norms[t] = jnp.zeros((8, 128), jnp.float32)
    loads = [
        load(0, grads, mine),
        load(1, right_root, root_all.at[:, whole(t)]),
        load(2, second, second_out),
        load(3, left_root, root_left),
        load(4, left_stat, left_out),
        load(5, right_stat, right_out),
    ]
    loads[0].start()

    barrier = pltpu.get_barrier_semaphore()
    for peer in (peer_x, peer_s, peer_y, peer_f):
        pl.semaphore_signal(barrier, inc=1, device_id=peer, device_id_type=MESH)
    pl.semaphore_wait(barrier, 4)

    go_x(0)
    go_x(1)
    go_root(0)
    go_x(2)
    go_x(3)
    for copy in loads[1:]:
        copy.start()
    go(B5, right_root, root_all.at[:, whole(t)], peer_s)

    def add(block, r):
        def body(i, carry):
            at = pl.ds(pl.multiple_of(r * chunk + i * 16, 16), 16)
            to = pl.ds(pl.multiple_of(t * rows + r * chunk + i * 16, 16), 16)
            total = mine[block, at].astype(jnp.float32) + theirs[block, at].astype(jnp.float32)
            summed[block, to] = total.astype(jnp.bfloat16)
            return carry

        lax.fori_loop(0, chunk // 16, body, 0, unroll=3)

    owners = [owner[b] for b in range(blocks)]
    weights = []
    for c in range(CAP):
        row = []
        for b in range(blocks):
            if b < c:
                row.append(None)
                continue
            rank = sum(((owners[e] == owners[b]).astype(jnp.int32) for e in range(b)), jnp.int32(0))
            row.append(((owners[b] == d) & (rank == c)).astype(jnp.float32))
        weights.append(row)

    def select(first, count):
        def body(i, carry):
            at = pl.ds(pl.multiple_of(first + i * 16, 16), 16)
            terms = [summed[b, at].astype(jnp.float32) for b in range(blocks)]
            for c in range(CAP):
                total = sum(terms[b] * weights[c][b] for b in range(c, blocks))
                gradient[c, at] = total.astype(jnp.bfloat16)
            return carry

        lax.fori_loop(0, count // 16, body, 0, unroll=3)

    loads[0].wait()
    for r in range(CHUNKS):
        arrived(X1 + r, theirs.at[d, pl.ds(r * chunk, chunk)], peer_x)
        add(d, r)
        go_rows(Y1 + r, d, place(t, r), peer_y)
    go_root(1)
    go_rows(B1, d, whole(t), peer_s)
    for r in range(CHUNKS):
        arrived(X2 + r, theirs.at[other, pl.ds(r * chunk, chunk)], peer_x)
        add(other, r)
        if r == CHUNKS - 1:
            go_rows(B2, other, whole(t), peer_s)
        arrived(Y1 + r, summed.at[d, place(across, r)], peer_y)
        go_rows(X3 + r, d, place(across, r), peer_x)
    go_rows(B3, d, whole(across), peer_s)

    select(t * rows, rows)
    loads[2].wait()
    for c in range(CAP):

        def moment(i, total):
            at = pl.ds(pl.multiple_of(i * 16, 16), 16)
            g = gradient[c, pl.ds(pl.multiple_of(t * rows + i * 16, 16), 16)].astype(jnp.float32)
            new = 0.9 * second_out[c, at] + 0.1 * g * g
            second_out[c, at] = new
            adam = g / (jnp.sqrt(new) + 1e-08)
            return total + fold(adam * adam)

        norms[t, c : c + 1] = jnp.sum(
            lax.fori_loop(0, rows // 16, moment, jnp.zeros((8, 128), jnp.float32), unroll=2),
            axis=0, keepdims=True,
        )
    root_came(0)

    near = pl.ds(pl.multiple_of(t // 2 * 2 * rows, 128), 2 * rows)
    away = pl.ds(pl.multiple_of((1 - t // 2) * 2 * rows, 128), 2 * rows)
    window = pl.ds(pl.multiple_of(128 * ((3 * t) // 2), 128), tile)
    shift = pl.ds(pl.multiple_of(64 * (t % 2), 64), rows)

    def tiled(body):
        def step(i, carry):
            body(i // tiles, pl.ds(pl.multiple_of((i % tiles) * tile, tile), tile))
            return carry

        lax.fori_loop(0, CAP * tiles, step, 0)

    def turn(at):
        for c in range(CAP):
            window_t[c, :, at] = gradient[c, at, window].T
            turned[c, :, at] = window_t[c, shift, at]

    def left(at):
        def step(c, carry):
            product = lax.dot_general(
                gradient[c, whole(t)], gradient[c, at], (((1,), (1,)), ((), ())),
                preferred_element_type=jnp.float32,
            )
            left_out[c, :, at] = 0.95 * left_out[c, :, at] + 0.05 * product
            return carry

        lax.fori_loop(0, CAP, step, 0)

    def dot(a, b):
        return jnp.dot(a, b, preferred_element_type=jnp.float32)

    def mix_near(c, cut):
        mixed_sum[c, :, cut] = dot(root_left[c, :, near], gradient[c, near, cut])

    def mix_away(c, cut):
        product = dot(root_left[c, :, away], gradient[c, away, cut])
        mixed[c, :, cut] = (mixed_sum[c, :, cut] + product).astype(jnp.bfloat16)

    def right_near(c, cut):
        right_sum[c, :, cut] = dot(turned[c, :, near], gradient[c, near, cut])

    def right_away(c, cut):
        product = right_sum[c, :, cut] + dot(turned[c, :, away], gradient[c, away, cut])
        right_out[c, :, cut] = 0.95 * right_out[c, :, cut] + 0.05 * product

    arrived(B1, summed.at[d, whole(sibling)], peer_s)
    arrived(B2, summed.at[other, whole(sibling)], peer_s)
    select(sibling * rows, rows)
    loads[3].wait()
    tiled(mix_near)
    for r in range(CHUNKS):
        arrived(X3 + r, summed.at[other, place(across, r)], peer_x)
        go_rows(B4 + r, other, place(across, r), peer_s)
        select(across * rows + r * chunk, chunk)
        if r == 0:
            turn(near)
            tiled(right_near)
            loads[4].wait()
            left(near)
    arrived(B3, summed.at[d, whole(far)], peer_s)
    for r in range(CHUNKS):
        arrived(B4 + r, summed.at[other, place(far, r)], peer_s)
        select(far * rows + r * chunk, chunk)
    root_came(1)
    tiled(mix_away)
    loads[1].wait()
    arrived(B5, root_all.at[:, whole(sibling)], peer_s)
    for c in range(CAP):
        arrived(B6 + c, root_part(far, c), peer_s)

        def multiply(i, total):
            cut = pl.ds(pl.multiple_of(i * tile, tile), tile)
            product = dot(mixed[c], root_all[c, :, cut])
            precond[c, :, cut] = product
            return total + fold(product * product)

        norms[t, CAP + c : CAP + c + 1] = jnp.sum(
            lax.fori_loop(0, tiles, multiply, jnp.zeros((8, 128), jnp.float32)),
            axis=0, keepdims=True,
        )
    for k, peer in enumerate((peer_s, peer_y, peer_f)):
        go(Z + k, norms.at[t], norms.at[t], peer)

    left(away)
    turn(away)
    loads[5].wait()
    tiled(right_away)
    for copy in sent:
        copy.wait_send()
    for k, (rank, peer) in enumerate(((sibling, peer_s), (across, peer_y), (far, peer_f))):
        arrived(Z + k, norms.at[rank], peer)
    totals[...] = norms[0] + norms[1] + norms[2] + norms[3]


def finish(
    left, right, second, precond, totals,
    left_out, right_out, second_out, direction_out, direction, sems,
):
    rows = precond.shape[1]
    pairs = ((left, left_out), (right, right_out), (second, second_out))
    copies = [pltpu.make_async_copy(a, b, sems.at[k]) for k, (a, b) in enumerate(pairs)]
    for copy in copies:
        copy.start()
    total = jnp.sum(totals[...], axis=1, keepdims=True)
    for c in range(CAP):
        scaling = jnp.sqrt(total[c : c + 1]) / jnp.sqrt(total[CAP + c : CAP + c + 1] + 1e-06)

        def scale(i, carry):
            at = pl.ds(pl.multiple_of(i * 16, 16), 16)
            direction[c, at] = (precond[c, at] * scaling).astype(jnp.bfloat16)
            return carry

        lax.fori_loop(0, rows // 16, scale, 0, unroll=2)
        copies.append(
            pltpu.make_async_copy(direction.at[c], direction_out.at[c], sems.at[3 + c])
        )
        copies[-1].start()
    for copy in copies:
        copy.wait()


def fused_step(grads, owner, left_stat, right_stat, second_moment, left_root, right_root):
    _, blocks, rows, width = grads.shape
    full = (CAP, width, width)
    part = (CAP, rows, width)
    f32, bf16 = jnp.float32, jnp.bfloat16
    outside, inside = pl.BlockSpec(memory_space=pltpu.HBM), pl.BlockSpec(memory_space=pltpu.VMEM)
    big, small = jax.ShapeDtypeStruct(part, f32), jax.ShapeDtypeStruct((8, 128), f32)
    parts = pl.pallas_call(
        kernel,
        out_shape=[big] * 4 + [small],
        in_specs=[pl.BlockSpec(memory_space=pltpu.SMEM)] + [outside] * 6,
        out_specs=[inside] * 5,
        scratch_shapes=[
            pltpu.VMEM((blocks, rows, width), bf16),
            pltpu.VMEM((blocks, rows, width), bf16),
            pltpu.VMEM((blocks, width, width), bf16),
            pltpu.VMEM(full, bf16),
            pltpu.VMEM(full, bf16),
            pltpu.VMEM(part, bf16),
            pltpu.VMEM(part, bf16),
            pltpu.VMEM(part, bf16),
            pltpu.VMEM((CAP, 256, width), bf16),
            pltpu.VMEM(part, f32),
            pltpu.VMEM(part, f32),
            pltpu.VMEM((4, 8, 128), f32),
            pltpu.SemaphoreType.DMA((6,)),
            pltpu.SemaphoreType.DMA((Z + 3,)),
            pltpu.SemaphoreType.DMA((Z + 3,)),
        ],
        compiler_params=pltpu.CompilerParams(
            collective_id=0, has_side_effects=True, vmem_limit_bytes=32 * 1024 * 1024
        ),
    )(
        owner.reshape(blocks),
        *(
            pltpu.with_memory_space_constraint(x, pltpu.HBM)
            for x in (
                grads[0], left_stat[0, 0], right_stat[0, 0], second_moment[0, 0],
                left_root[0, 0], right_root[0, 0],
            )
        ),
    )
    outs = pl.pallas_call(
        finish,
        out_shape=[big] * 3 + [jax.ShapeDtypeStruct(part, bf16)],
        in_specs=[pl.BlockSpec(memory_space=pl.ANY)] * 3 + [inside] * 2,
        out_specs=[outside] * 4,
        scratch_shapes=[pltpu.VMEM(part, bf16), pltpu.SemaphoreType.DMA((3 + CAP,))],
        compiler_params=pltpu.CompilerParams(vmem_limit_bytes=16 * 1024 * 1024),
    )(*parts)
    return tuple(out[None, None] for out in outs)


def solution(mesh):
    state = P("dp", "section", None, "tensor", None)
    placed = (P("dp", "section", "tensor", None), P("section", None)) + (state,) * 5

    def step(*args):
        _, blocks, rows, width = args[0].shape
        fits = mesh.shape["dp"] == 2 and mesh.shape["tensor"] == 4 and blocks == 2
        fits = fits and rows == 192 and width == 768 and args[2].shape[2] == CAP
        return (fused_step if fits else plain_step)(*args)

    return jax.shard_map(
        step, mesh=mesh, in_specs=placed, out_specs=(state,) * 4, check_vma=False
    )
```

```python
import functools

import jax
import jax.numpy as jnp
from jax import lax
from jax.experimental import pallas as pl
from jax.experimental.pallas import tpu as pltpu
from jax.sharding import PartitionSpec as P

CAP = 2
MESH = pl.DeviceIdType.MESH

CHUNKS = 2
X1, X2, X3, Y1, B4, B6, B1, B2, B3, B5, Y2, Z = (*range(0, 12, 2), *range(12, 17), 20)


def plain_step(grads, owner, left_stat, right_stat, second_moment, left_root, right_root):
    block_count = owner.shape[0]
    my_rank = lax.axis_index("dp")
    owners_list = owner[:, 0]
    positions = jnp.arange(block_count, dtype=jnp.int32)
    same_owner = owners_list[:, None] == owners_list[None, :]
    earlier = positions[None, :] < positions[:, None]
    ranked = jnp.sum((same_owner & earlier).astype(jnp.int32), axis=1)
    slot_ids = jnp.arange(CAP, dtype=jnp.int32)
    local_grads = grads[0]
    chosen = (owners_list[None, :] == my_rank) & (ranked[None, :] == slot_ids[:, None])
    index_table = jnp.sum(chosen.astype(jnp.int32) * positions[None, :], axis=1)
    occupied = jnp.any(chosen, axis=1).astype(jnp.float32)
    summed = lax.psum(local_grads.astype(jnp.float32).astype(jnp.bfloat16), "dp").astype(
        jnp.float32
    )
    slot_sum = jnp.take(summed, index_table, axis=0) * occupied[:, None, None]
    gradient = slot_sum.astype(jnp.bfloat16)
    gathered = lax.all_gather(gradient, "tensor", axis=1, tiled=True)
    left_incr = jnp.einsum("cik,cjk->cij", gradient, gathered, preferred_element_type=jnp.float32)
    left_new = 0.95 * left_stat[0, 0] + 0.05 * left_incr
    partials = jnp.einsum("cki,ckj->cij", gradient, gradient, preferred_element_type=jnp.float32)
    right_incr = lax.psum_scatter(
        partials.astype(jnp.bfloat16), "tensor", scatter_dimension=1, tiled=True
    ).astype(jnp.float32)
    right_new = 0.95 * right_stat[0, 0] + 0.05 * right_incr
    grad_wide = gradient.astype(jnp.float32)
    second_new = 0.9 * second_moment[0, 0] + 0.1 * grad_wide * grad_wide
    adam_dir = grad_wide / (jnp.sqrt(second_new) + 1e-08)
    mixed = jnp.einsum(
        "cik,ckj->cij", left_root[0, 0], gathered, preferred_element_type=jnp.float32
    ).astype(jnp.bfloat16)
    precond = jnp.einsum(
        "cik,ckj->cij",
        mixed,
        lax.all_gather(right_root[0, 0], "tensor", axis=1, tiled=True),
        preferred_element_type=jnp.float32,
    )
    precond_sq = jnp.sum(precond * precond, axis=(1, 2))
    adam_sq = jnp.sum(adam_dir * adam_dir, axis=(1, 2))
    precond_sq, adam_sq = lax.psum((precond_sq, adam_sq), "tensor")
    scaling = jnp.sqrt(adam_sq) / jnp.sqrt(precond_sq + 1e-06)
    direction = (precond * scaling[:, None, None]).astype(jnp.bfloat16)
    return (
        left_new[None, None],
        right_new[None, None],
        second_new[None, None],
        direction[None, None],
    )


def fold(values):
    rows, columns = values.shape
    total = jnp.sum(values.reshape(rows // 8, 8, columns), axis=0)
    return sum(total[:, i : i + 128] for i in range(0, columns, 128))


def kernel(
    owner, grads, left_stat, right_stat, second, left_root, right_root,
    left_out, right_out, second_out, precond, totals,
    mine, theirs, summed, gradient, root_all, root_left,
    mixed, turned, window_t, mixed_sum, right_sum, norms, local_sem, send_sem, recv_sem,
):
    d, t = lax.axis_index("dp"), lax.axis_index("tensor")
    blocks, rows, width = mine.shape
    chunk, half, tile = rows // CHUNKS, rows // 2, 256
    tiles = width // tile
    other = 1 - d
    sibling, across, far = t + 1 - 2 * (t % 2), (t + 2) % 4, 3 - t
    peer_x, peer_s, peer_y = {"dp": other}, {"tensor": sibling}, {"tensor": across}
    peer_f = {"tensor": far}

    def load(k, source, target):
        return pltpu.make_async_copy(source, target, local_sem.at[k])

    def place(rank, r):
        return pl.ds(pl.multiple_of(rank * rows + r * chunk, 16), chunk)

    def whole(rank):
        return pl.ds(pl.multiple_of(rank * rows, 16), rows)

    def root_part(rank, c):
        return root_all.at[c, whole(rank)]

    def send(k, source, target, device):
        return pltpu.make_async_remote_copy(
            src_ref=source, dst_ref=target, send_sem=send_sem.at[k], recv_sem=recv_sem.at[k],
            device_id=device, device_id_type=MESH,
        )

    def go(k, source, target, device):
        copy = send(k, source, target, device)
        copy.start()
        sent.append(copy)

    def arrived(k, target, device):
        send(k, target, target, device).wait_recv()

    def go_rows(k, block, at, device):
        go(k, summed.at[block, at], summed.at[block, at], device)

    def go_x(k):
        block, part = (other, d)[k // CHUNKS], pl.ds(k % CHUNKS * chunk, chunk)
        go(X1 + k, grads.at[block, part], theirs.at[block, part], peer_x)

    def root_half(rank, k):
        return root_all.at[k // 2, pl.ds(pl.multiple_of(rank * rows + k % 2 * half, 16), half)]

    def go_root(k):
        go(Y2 + k, right_root.at[k // 2, pl.ds(k % 2 * half, half)], root_half(t, k), peer_y)

    def root_came(c):
        for k in (2 * c, 2 * c + 1):
            arrived(Y2 + k, root_half(across, k), peer_y)
        go(B6 + c, root_part(across, c), root_part(across, c), peer_s)

    sent = []
    norms[t] = jnp.zeros((8, 128), jnp.float32)
    loads = [
        load(0, grads, mine),
        load(1, right_root, root_all.at[:, whole(t)]),
        load(2, second, second_out),
        load(3, left_root, root_left),
        load(4, left_stat, left_out),
        load(5, right_stat, right_out),
    ]
    loads[0].start()

    barrier = pltpu.get_barrier_semaphore()
    for peer in (peer_x, peer_s, peer_y, peer_f):
        pl.semaphore_signal(barrier, inc=1, device_id=peer, device_id_type=MESH)
    pl.semaphore_wait(barrier, 4)

    go_x(0)
    go_x(1)
    go_root(0)
    for copy in loads[1:]:
        copy.start()
    go(B5, right_root, root_all.at[:, whole(t)], peer_s)

    def add(block, r):
        def body(i, carry):
            at = pl.ds(pl.multiple_of(r * chunk + i * 16, 16), 16)
            to = pl.ds(pl.multiple_of(t * rows + r * chunk + i * 16, 16), 16)
            total = mine[block, at].astype(jnp.float32) + theirs[block, at].astype(jnp.float32)
            summed[block, to] = total.astype(jnp.bfloat16)
            return carry

        lax.fori_loop(0, chunk // 16, body, 0, unroll=3)

    owners = [owner[b] for b in range(blocks)]
    weights = []
    for c in range(CAP):
        row = []
        for b in range(blocks):
            if b < c:
                row.append(None)
                continue
            rank = sum(((owners[e] == owners[b]).astype(jnp.int32) for e in range(b)), jnp.int32(0))
            row.append(((owners[b] == d) & (rank == c)).astype(jnp.float32))
        weights.append(row)

    def select(first, count):
        def body(i, carry):
            at = pl.ds(pl.multiple_of(first + i * 16, 16), 16)
            terms = [summed[b, at].astype(jnp.float32) for b in range(blocks)]
            for c in range(CAP):
                total = sum(terms[b] * weights[c][b] for b in range(c, blocks))
                gradient[c, at] = total.astype(jnp.bfloat16)
            return carry

        lax.fori_loop(0, count // 16, body, 0, unroll=3)

    loads[0].wait()
    for r in range(CHUNKS):
        arrived(X1 + r, theirs.at[d, pl.ds(r * chunk, chunk)], peer_x)
        go_x(CHUNKS + r)
        add(d, r)
        go_rows(Y1 + r, d, place(t, r), peer_y)
    go_rows(B1, d, whole(t), peer_s)
    for r in range(CHUNKS):
        arrived(Y1 + r, summed.at[d, place(across, r)], peer_y)
        go_rows(X3 + r, d, place(across, r), peer_x)
        go_root(1 + r)
        if r == CHUNKS - 1:
            go_root(3)
        arrived(X2 + r, theirs.at[other, pl.ds(r * chunk, chunk)], peer_x)
        add(other, r)
    go_rows(B2, other, whole(t), peer_s)
    go_rows(B3, d, whole(across), peer_s)

    select(t * rows, rows)
    loads[2].wait()
    for c in range(CAP):

        def moment(i, total):
            at = pl.ds(pl.multiple_of(i * 16, 16), 16)
            g = gradient[c, pl.ds(pl.multiple_of(t * rows + i * 16, 16), 16)].astype(jnp.float32)
            new = 0.9 * second_out[c, at] + 0.1 * g * g
            second_out[c, at] = new
            adam = g / (jnp.sqrt(new) + 1e-08)
            return total + fold(adam * adam)

        norms[t, c : c + 1] = jnp.sum(
            lax.fori_loop(0, rows // 16, moment, jnp.zeros((8, 128), jnp.float32), unroll=2),
            axis=0, keepdims=True,
        )
    root_came(0)

    near = pl.ds(pl.multiple_of(t // 2 * 2 * rows, 128), 2 * rows)
    away = pl.ds(pl.multiple_of((1 - t // 2) * 2 * rows, 128), 2 * rows)
    window = pl.ds(pl.multiple_of(128 * ((3 * t) // 2), 128), tile)
    shift = pl.ds(pl.multiple_of(64 * (t % 2), 64), rows)

    def tiled(body):
        def step(i, carry):
            body(i // tiles, pl.ds(pl.multiple_of((i % tiles) * tile, tile), tile))
            return carry

        lax.fori_loop(0, CAP * tiles, step, 0)

    def turn(at):
        for c in range(CAP):
            window_t[c, :, at] = gradient[c, at, window].T
            turned[c, :, at] = window_t[c, shift, at]

    def left(at):
        def step(c, carry):
            product = lax.dot_general(
                gradient[c, whole(t)], gradient[c, at], (((1,), (1,)), ((), ())),
                preferred_element_type=jnp.float32,
            )
            left_out[c, :, at] = 0.95 * left_out[c, :, at] + 0.05 * product
            return carry

        lax.fori_loop(0, CAP, step, 0)

    def dot(a, b):
        return jnp.dot(a, b, preferred_element_type=jnp.float32)

    def mix_near(c, cut):
        mixed_sum[c, :, cut] = dot(root_left[c, :, near], gradient[c, near, cut])

    def mix_away(c, cut):
        product = dot(root_left[c, :, away], gradient[c, away, cut])
        mixed[c, :, cut] = (mixed_sum[c, :, cut] + product).astype(jnp.bfloat16)

    def right_near(c, cut):
        right_sum[c, :, cut] = dot(turned[c, :, near], gradient[c, near, cut])

    def right_away(c, cut):
        product = right_sum[c, :, cut] + dot(turned[c, :, away], gradient[c, away, cut])
        right_out[c, :, cut] = 0.95 * right_out[c, :, cut] + 0.05 * product

    arrived(B1, summed.at[d, whole(sibling)], peer_s)
    arrived(B2, summed.at[other, whole(sibling)], peer_s)
    select(sibling * rows, rows)
    loads[3].wait()
    tiled(mix_near)
    for r in range(CHUNKS):
        arrived(X3 + r, summed.at[other, place(across, r)], peer_x)
        go_rows(B4 + r, other, place(across, r), peer_s)
        select(across * rows + r * chunk, chunk)
        if r == 0:
            turn(near)
            tiled(right_near)
            loads[4].wait()
            left(near)
    arrived(B3, summed.at[d, whole(far)], peer_s)
    for r in range(CHUNKS):
        arrived(B4 + r, summed.at[other, place(far, r)], peer_s)
        select(far * rows + r * chunk, chunk)
    root_came(1)
    tiled(mix_away)
    loads[1].wait()
    arrived(B5, root_all.at[:, whole(sibling)], peer_s)
    for c in range(CAP):
        arrived(B6 + c, root_part(far, c), peer_s)

        def multiply(i, total):
            cut = pl.ds(pl.multiple_of(i * tile, tile), tile)
            product = dot(mixed[c], root_all[c, :, cut])
            precond[c, :, cut] = product
            return total + fold(product * product)

        norms[t, CAP + c : CAP + c + 1] = jnp.sum(
            lax.fori_loop(0, tiles, multiply, jnp.zeros((8, 128), jnp.float32)),
            axis=0, keepdims=True,
        )
    for k, peer in enumerate((peer_s, peer_y, peer_f)):
        go(Z + k, norms.at[t], norms.at[t], peer)

    left(away)
    turn(away)
    loads[5].wait()
    tiled(right_away)
    for copy in sent:
        copy.wait_send()
    for k, (rank, peer) in enumerate(((sibling, peer_s), (across, peer_y), (far, peer_f))):
        arrived(Z + k, norms.at[rank], peer)
    totals[...] = norms[0] + norms[1] + norms[2] + norms[3]


def finish(
    left, right, second, precond, totals,
    left_out, right_out, second_out, direction_out, direction, sems,
):
    rows = precond.shape[1]
    pairs = ((left, left_out), (right, right_out), (second, second_out))
    copies = [pltpu.make_async_copy(a, b, sems.at[k]) for k, (a, b) in enumerate(pairs)]
    for copy in copies:
        copy.start()
    total = jnp.sum(totals[...], axis=1, keepdims=True)
    for c in range(CAP):
        scaling = jnp.sqrt(total[c : c + 1]) / jnp.sqrt(total[CAP + c : CAP + c + 1] + 1e-06)

        def scale(i, carry):
            at = pl.ds(pl.multiple_of(i * 16, 16), 16)
            direction[c, at] = (precond[c, at] * scaling).astype(jnp.bfloat16)
            return carry

        lax.fori_loop(0, rows // 16, scale, 0, unroll=2)
        copies.append(
            pltpu.make_async_copy(direction.at[c], direction_out.at[c], sems.at[3 + c])
        )
        copies[-1].start()
    for copy in copies:
        copy.wait()


def fused_step(grads, owner, left_stat, right_stat, second_moment, left_root, right_root):
    _, blocks, rows, width = grads.shape
    full = (CAP, width, width)
    part = (CAP, rows, width)
    f32, bf16 = jnp.float32, jnp.bfloat16
    outside, inside = pl.BlockSpec(memory_space=pltpu.HBM), pl.BlockSpec(memory_space=pltpu.VMEM)
    big, small = jax.ShapeDtypeStruct(part, f32), jax.ShapeDtypeStruct((8, 128), f32)
    parts = pl.pallas_call(
        kernel,
        out_shape=[big] * 4 + [small],
        in_specs=[pl.BlockSpec(memory_space=pltpu.SMEM)] + [outside] * 6,
        out_specs=[inside] * 5,
        scratch_shapes=[
            pltpu.VMEM((blocks, rows, width), bf16),
            pltpu.VMEM((blocks, rows, width), bf16),
            pltpu.VMEM((blocks, width, width), bf16),
            pltpu.VMEM(full, bf16),
            pltpu.VMEM(full, bf16),
            pltpu.VMEM(part, bf16),
            pltpu.VMEM(part, bf16),
            pltpu.VMEM(part, bf16),
            pltpu.VMEM((CAP, 256, width), bf16),
            pltpu.VMEM(part, f32),
            pltpu.VMEM(part, f32),
            pltpu.VMEM((4, 8, 128), f32),
            pltpu.SemaphoreType.DMA((6,)),
            pltpu.SemaphoreType.DMA((Z + 3,)),
            pltpu.SemaphoreType.DMA((Z + 3,)),
        ],
        compiler_params=pltpu.CompilerParams(
            collective_id=0, has_side_effects=True, vmem_limit_bytes=32 * 1024 * 1024
        ),
    )(
        owner.reshape(blocks),
        *(
            pltpu.with_memory_space_constraint(x, pltpu.HBM)
            for x in (
                grads[0], left_stat[0, 0], right_stat[0, 0], second_moment[0, 0],
                left_root[0, 0], right_root[0, 0],
            )
        ),
    )
    outs = pl.pallas_call(
        finish,
        out_shape=[big] * 3 + [jax.ShapeDtypeStruct(part, bf16)],
        in_specs=[pl.BlockSpec(memory_space=pl.ANY)] * 3 + [inside] * 2,
        out_specs=[outside] * 4,
        scratch_shapes=[pltpu.VMEM(part, bf16), pltpu.SemaphoreType.DMA((3 + CAP,))],
        compiler_params=pltpu.CompilerParams(vmem_limit_bytes=16 * 1024 * 1024),
    )(*parts)
    return tuple(out[None, None] for out in outs)


def solution(mesh):
    state = P("dp", "section", None, "tensor", None)
    placed = (P("dp", "section", "tensor", None), P("section", None)) + (state,) * 5

    def step(*args):
        _, blocks, rows, width = args[0].shape
        fits = mesh.shape["dp"] == 2 and mesh.shape["tensor"] == 4 and blocks == 2
        fits = fits and rows == 192 and width == 768 and args[2].shape[2] == CAP
        return (fused_step if fits else plain_step)(*args)

    return jax.shard_map(
        step, mesh=mesh, in_specs=placed, out_specs=(state,) * 4, check_vma=False
    )
```

```python
import functools

import jax
import jax.numpy as jnp
from jax import lax
from jax.experimental import pallas as pl
from jax.experimental.pallas import tpu as pltpu
from jax.sharding import PartitionSpec as P

CAP = 2
MESH = pl.DeviceIdType.MESH

CHUNKS = 2
X1, X2, X3, Y1, B4, B6, B1, B2, B3, B5, Y3, Y2, Z = (*range(0, 12, 2), *range(12, 18), 20)


def plain_step(grads, owner, left_stat, right_stat, second_moment, left_root, right_root):
    block_count = owner.shape[0]
    my_rank = lax.axis_index("dp")
    owners_list = owner[:, 0]
    positions = jnp.arange(block_count, dtype=jnp.int32)
    same_owner = owners_list[:, None] == owners_list[None, :]
    earlier = positions[None, :] < positions[:, None]
    ranked = jnp.sum((same_owner & earlier).astype(jnp.int32), axis=1)
    slot_ids = jnp.arange(CAP, dtype=jnp.int32)
    local_grads = grads[0]
    chosen = (owners_list[None, :] == my_rank) & (ranked[None, :] == slot_ids[:, None])
    index_table = jnp.sum(chosen.astype(jnp.int32) * positions[None, :], axis=1)
    occupied = jnp.any(chosen, axis=1).astype(jnp.float32)
    summed = lax.psum(local_grads.astype(jnp.float32).astype(jnp.bfloat16), "dp").astype(
        jnp.float32
    )
    slot_sum = jnp.take(summed, index_table, axis=0) * occupied[:, None, None]
    gradient = slot_sum.astype(jnp.bfloat16)
    gathered = lax.all_gather(gradient, "tensor", axis=1, tiled=True)
    left_incr = jnp.einsum("cik,cjk->cij", gradient, gathered, preferred_element_type=jnp.float32)
    left_new = 0.95 * left_stat[0, 0] + 0.05 * left_incr
    partials = jnp.einsum("cki,ckj->cij", gradient, gradient, preferred_element_type=jnp.float32)
    right_incr = lax.psum_scatter(
        partials.astype(jnp.bfloat16), "tensor", scatter_dimension=1, tiled=True
    ).astype(jnp.float32)
    right_new = 0.95 * right_stat[0, 0] + 0.05 * right_incr
    grad_wide = gradient.astype(jnp.float32)
    second_new = 0.9 * second_moment[0, 0] + 0.1 * grad_wide * grad_wide
    adam_dir = grad_wide / (jnp.sqrt(second_new) + 1e-08)
    mixed = jnp.einsum(
        "cik,ckj->cij", left_root[0, 0], gathered, preferred_element_type=jnp.float32
    ).astype(jnp.bfloat16)
    precond = jnp.einsum(
        "cik,ckj->cij",
        mixed,
        lax.all_gather(right_root[0, 0], "tensor", axis=1, tiled=True),
        preferred_element_type=jnp.float32,
    )
    precond_sq = jnp.sum(precond * precond, axis=(1, 2))
    adam_sq = jnp.sum(adam_dir * adam_dir, axis=(1, 2))
    precond_sq, adam_sq = lax.psum((precond_sq, adam_sq), "tensor")
    scaling = jnp.sqrt(adam_sq) / jnp.sqrt(precond_sq + 1e-06)
    direction = (precond * scaling[:, None, None]).astype(jnp.bfloat16)
    return (
        left_new[None, None],
        right_new[None, None],
        second_new[None, None],
        direction[None, None],
    )


def fold(values):
    rows, columns = values.shape
    total = jnp.sum(values.reshape(rows // 8, 8, columns), axis=0)
    return sum(total[:, i : i + 128] for i in range(0, columns, 128))


def kernel(
    owner, grads, left_stat, right_stat, second, left_root, right_root,
    left_out, right_out, second_out, precond, totals,
    mine, theirs, summed, gradient, root_all, root_left,
    mixed, turned, window_t, mixed_sum, right_sum, norms, owner_at, local_sem, send_sem, recv_sem,
):
    d, t = lax.axis_index("dp"), lax.axis_index("tensor")
    blocks, rows, width = mine.shape
    chunk, half, tile = rows // CHUNKS, rows // 2, 256
    tiles = width // tile
    other = 1 - d
    sibling, across, far = t + 1 - 2 * (t % 2), (t + 2) % 4, 3 - t
    peer_x, peer_s, peer_y = {"dp": other}, {"tensor": sibling}, {"tensor": across}
    peer_f = {"tensor": far}

    def load(k, source, target):
        return pltpu.make_async_copy(source, target, local_sem.at[k])

    def place(rank, r):
        return pl.ds(pl.multiple_of(rank * rows + r * chunk, 16), chunk)

    def whole(rank):
        return pl.ds(pl.multiple_of(rank * rows, 16), rows)

    def root_part(rank, c):
        return root_all.at[c, whole(rank)]

    def send(k, source, target, device):
        return pltpu.make_async_remote_copy(
            src_ref=source, dst_ref=target, send_sem=send_sem.at[k], recv_sem=recv_sem.at[k],
            device_id=device, device_id_type=MESH,
        )

    def go(k, source, target, device):
        copy = send(k, source, target, device)
        copy.start()
        sent.append(copy)

    def arrived(k, target, device):
        send(k, target, target, device).wait_recv()

    def go_rows(k, block, at, device):
        go(k, summed.at[block, at], summed.at[block, at], device)

    def go_x(k):
        block, part = (other, d)[k // CHUNKS], pl.ds(k % CHUNKS * chunk, chunk)
        go(X1 + k, grads.at[block, part], theirs.at[block, part], peer_x)

    def root_piece(rank, k):
        if k == 0:
            return root_part(rank, 0)
        at = pl.ds(pl.multiple_of(rank * rows + (k - 1) * half, 16), half)
        return root_all.at[1, at]

    def go_root(k):
        source = right_root.at[0] if k == 0 else right_root.at[1, pl.ds((k - 1) * half, half)]
        go(Y2 + k, source, root_piece(t, k), peer_y)

    def root_came(c):
        for k in ((0,), (1, 2))[c]:
            arrived(Y2 + k, root_piece(across, k), peer_y)
        go(B6 + c, root_part(across, c), root_part(across, c), peer_s)

    def quarter(rank, k):
        return pl.ds(pl.multiple_of(rank * rows + k * (chunk // 2), 16), chunk // 2)

    sent = []
    norms[t] = jnp.zeros((8, 128), jnp.float32)
    loads = [
        load(0, grads, mine),
        load(1, right_root, root_all.at[:, whole(t)]),
        load(2, second, second_out),
        load(3, left_root, root_left),
        load(4, left_stat, left_out),
        load(5, right_stat, right_out),
        load(6, owner, owner_at),
    ]
    loads[0].start()
    loads[6].start()

    barrier = pltpu.get_barrier_semaphore()
    for peer in (peer_x, peer_s, peer_y, peer_f):
        pl.semaphore_signal(barrier, inc=1, device_id=peer, device_id_type=MESH)
    pl.semaphore_wait(barrier, 4)

    go_x(0)
    go_x(1)
    go_root(0)
    go_x(2)
    go_x(3)
    for copy in loads[1:6]:
        copy.start()
    go(B5, right_root, root_all.at[:, whole(t)], peer_s)

    def add(block, r):
        def body(i, carry):
            at = pl.ds(pl.multiple_of(r * chunk + i * 16, 16), 16)
            to = pl.ds(pl.multiple_of(t * rows + r * chunk + i * 16, 16), 16)
            total = mine[block, at].astype(jnp.float32) + theirs[block, at].astype(jnp.float32)
            summed[block, to] = total.astype(jnp.bfloat16)
            return carry

        lax.fori_loop(0, chunk // 16, body, 0, unroll=3)

    loads[6].wait()
    owners = [owner_at[b] for b in range(blocks)]
    weights = []
    for c in range(CAP):
        row = []
        for b in range(blocks):
            if b < c:
                row.append(None)
                continue
            rank = sum(((owners[e] == owners[b]).astype(jnp.int32) for e in range(b)), jnp.int32(0))
            row.append(((owners[b] == d) & (rank == c)).astype(jnp.float32))
        weights.append(row)

    def select(first, count):
        def body(i, carry):
            at = pl.ds(pl.multiple_of(first + i * 16, 16), 16)
            terms = [summed[b, at].astype(jnp.float32) for b in range(blocks)]
            for c in range(CAP):
                total = sum(terms[b] * weights[c][b] for b in range(c, blocks))
                gradient[c, at] = total.astype(jnp.bfloat16)
            return carry

        lax.fori_loop(0, count // 16, body, 0, unroll=3)

    loads[0].wait()
    for r in range(CHUNKS):
        arrived(X1 + r, theirs.at[d, pl.ds(r * chunk, chunk)], peer_x)
        add(d, r)
        go_rows(Y1 + r, d, place(t, r), peer_y)
    go_root(1)
    go_rows(B1, d, whole(t), peer_s)
    for r in range(CHUNKS):
        arrived(X2 + r, theirs.at[other, pl.ds(r * chunk, chunk)], peer_x)
        add(other, r)
        if r == CHUNKS - 1:
            go_rows(B2, other, whole(t), peer_s)
            go_rows(Y3, other, quarter(t, 3), peer_y)
            go_root(2)
        arrived(Y1 + r, summed.at[d, place(across, r)], peer_y)
        go_rows(X3 + r, d, place(across, 0) if r == 0 else quarter(across, 2), peer_x)
    go_rows(B3, d, whole(across), peer_s)

    select(t * rows, rows)
    loads[2].wait()
    for c in range(CAP):

        def moment(i, total):
            at = pl.ds(pl.multiple_of(i * 16, 16), 16)
            g = gradient[c, pl.ds(pl.multiple_of(t * rows + i * 16, 16), 16)].astype(jnp.float32)
            new = 0.9 * second_out[c, at] + 0.1 * g * g
            second_out[c, at] = new
            adam = g / (jnp.sqrt(new) + 1e-08)
            return total + fold(adam * adam)

        norms[t, c : c + 1] = jnp.sum(
            lax.fori_loop(0, rows // 16, moment, jnp.zeros((8, 128), jnp.float32), unroll=2),
            axis=0, keepdims=True,
        )
    root_came(0)

    near = pl.ds(pl.multiple_of(t // 2 * 2 * rows, 128), 2 * rows)
    away = pl.ds(pl.multiple_of((1 - t // 2) * 2 * rows, 128), 2 * rows)
    window = pl.ds(pl.multiple_of(128 * ((3 * t) // 2), 128), tile)
    shift = pl.ds(pl.multiple_of(64 * (t % 2), 64), rows)

    def tiled(body):
        def step(i, carry):
            body(i // tiles, pl.ds(pl.multiple_of((i % tiles) * tile, tile), tile))
            return carry

        lax.fori_loop(0, CAP * tiles, step, 0)

    def turn(at):
        for c in range(CAP):
            window_t[c, :, at] = gradient[c, at, window].T
            turned[c, :, at] = window_t[c, shift, at]

    def left(at):
        def step(c, carry):
            product = lax.dot_general(
                gradient[c, whole(t)], gradient[c, at], (((1,), (1,)), ((), ())),
                preferred_element_type=jnp.float32,
            )
            left_out[c, :, at] = 0.95 * left_out[c, :, at] + 0.05 * product
            return carry

        lax.fori_loop(0, CAP, step, 0)

    def dot(a, b):
        return jnp.dot(a, b, preferred_element_type=jnp.float32)

    def mix_near(c, cut):
        mixed_sum[c, :, cut] = dot(root_left[c, :, near], gradient[c, near, cut])

    def mix_away(c, cut):
        product = dot(root_left[c, :, away], gradient[c, away, cut])
        mixed[c, :, cut] = (mixed_sum[c, :, cut] + product).astype(jnp.bfloat16)

    def right_near(c, cut):
        right_sum[c, :, cut] = dot(turned[c, :, near], gradient[c, near, cut])

    def right_away(c, cut):
        product = right_sum[c, :, cut] + dot(turned[c, :, away], gradient[c, away, cut])
        right_out[c, :, cut] = 0.95 * right_out[c, :, cut] + 0.05 * product

    arrived(B1, summed.at[d, whole(sibling)], peer_s)
    arrived(B2, summed.at[other, whole(sibling)], peer_s)
    select(sibling * rows, rows)
    loads[3].wait()
    tiled(mix_near)
    for r in range(CHUNKS):
        at = place(across, 0) if r == 0 else quarter(across, 2)
        arrived(X3 + r, summed.at[other, at], peer_x)
        if r == 1:
            arrived(Y3, summed.at[other, quarter(across, 3)], peer_y)
        go_rows(B4 + r, other, place(across, r), peer_s)
        select(across * rows + r * chunk, chunk)
        if r == 0:
            turn(near)
            tiled(right_near)
            loads[4].wait()
            left(near)
    arrived(B3, summed.at[d, whole(far)], peer_s)
    for r in range(CHUNKS):
        arrived(B4 + r, summed.at[other, place(far, r)], peer_s)
        select(far * rows + r * chunk, chunk)
    tiled(mix_away)
    loads[1].wait()
    arrived(B5, root_all.at[:, whole(sibling)], peer_s)
    for c in range(CAP):
        if c == 1:
            left(away)
            root_came(1)
        arrived(B6 + c, root_part(far, c), peer_s)

        def multiply(i, total):
            cut = pl.ds(pl.multiple_of(i * tile, tile), tile)
            product = dot(mixed[c], root_all[c, :, cut])
            precond[c, :, cut] = product
            return total + fold(product * product)

        norms[t, CAP + c : CAP + c + 1] = jnp.sum(
            lax.fori_loop(0, tiles, multiply, jnp.zeros((8, 128), jnp.float32)),
            axis=0, keepdims=True,
        )
    for k, peer in enumerate((peer_s, peer_y, peer_f)):
        go(Z + k, norms.at[t], norms.at[t], peer)

    turn(away)
    loads[5].wait()
    tiled(right_away)
    for copy in sent:
        copy.wait_send()
    for k, (rank, peer) in enumerate(((sibling, peer_s), (across, peer_y), (far, peer_f))):
        arrived(Z + k, norms.at[rank], peer)
    totals[...] = norms[0] + norms[1] + norms[2] + norms[3]


def finish(
    left, right, second, precond, totals,
    left_out, right_out, second_out, direction_out, direction, sems,
):
    rows = precond.shape[1]
    pairs = ((left, left_out), (right, right_out), (second, second_out))
    copies = [pltpu.make_async_copy(a, b, sems.at[k]) for k, (a, b) in enumerate(pairs)]
    for copy in copies:
        copy.start()
    total = jnp.sum(totals[...], axis=1, keepdims=True)
    for c in range(CAP):
        scaling = jnp.sqrt(total[c : c + 1]) / jnp.sqrt(total[CAP + c : CAP + c + 1] + 1e-06)

        def scale(i, carry):
            at = pl.ds(pl.multiple_of(i * 16, 16), 16)
            direction[c, at] = (precond[c, at] * scaling).astype(jnp.bfloat16)
            return carry

        lax.fori_loop(0, rows // 16, scale, 0, unroll=2)
        copies.append(
            pltpu.make_async_copy(direction.at[c], direction_out.at[c], sems.at[3 + c])
        )
        copies[-1].start()
    for copy in copies:
        copy.wait()


def fused_step(grads, owner, left_stat, right_stat, second_moment, left_root, right_root):
    _, blocks, rows, width = grads.shape
    full = (CAP, width, width)
    part = (CAP, rows, width)
    f32, bf16 = jnp.float32, jnp.bfloat16
    outside, inside = pl.BlockSpec(memory_space=pltpu.HBM), pl.BlockSpec(memory_space=pltpu.VMEM)
    big, small = jax.ShapeDtypeStruct(part, f32), jax.ShapeDtypeStruct((8, 128), f32)
    parts = pl.pallas_call(
        kernel,
        out_shape=[big] * 4 + [small],
        in_specs=[outside] * 7,
        out_specs=[inside] * 5,
        scratch_shapes=[
            pltpu.VMEM((blocks, rows, width), bf16),
            pltpu.VMEM((blocks, rows, width), bf16),
            pltpu.VMEM((blocks, width, width), bf16),
            pltpu.VMEM(full, bf16),
            pltpu.VMEM(full, bf16),
            pltpu.VMEM(part, bf16),
            pltpu.VMEM(part, bf16),
            pltpu.VMEM(part, bf16),
            pltpu.VMEM((CAP, 256, width), bf16),
            pltpu.VMEM(part, f32),
            pltpu.VMEM(part, f32),
            pltpu.VMEM((4, 8, 128), f32),
            pltpu.SMEM((blocks,), jnp.int32),
            pltpu.SemaphoreType.DMA((7,)),
            pltpu.SemaphoreType.DMA((Z + 3,)),
            pltpu.SemaphoreType.DMA((Z + 3,)),
        ],
        compiler_params=pltpu.CompilerParams(
            collective_id=0, has_side_effects=True, vmem_limit_bytes=32 * 1024 * 1024
        ),
    )(
        *(
            pltpu.with_memory_space_constraint(x, pltpu.HBM)
            for x in (
                owner.reshape(blocks), grads[0], left_stat[0, 0], right_stat[0, 0], second_moment[0, 0],
                left_root[0, 0], right_root[0, 0],
            )
        ),
    )
    outs = pl.pallas_call(
        finish,
        out_shape=[big] * 3 + [jax.ShapeDtypeStruct(part, bf16)],
        in_specs=[pl.BlockSpec(memory_space=pl.ANY)] * 3 + [inside] * 2,
        out_specs=[outside] * 4,
        scratch_shapes=[pltpu.VMEM(part, bf16), pltpu.SemaphoreType.DMA((3 + CAP,))],
        compiler_params=pltpu.CompilerParams(vmem_limit_bytes=16 * 1024 * 1024),
    )(*parts)
    return tuple(out[None, None] for out in outs)


def solution(mesh):
    state = P("dp", "section", None, "tensor", None)
    placed = (P("dp", "section", "tensor", None), P("section", None)) + (state,) * 5

    def step(*args):
        _, blocks, rows, width = args[0].shape
        fits = mesh.shape["dp"] == 2 and mesh.shape["tensor"] == 4 and blocks == 2
        fits = fits and rows == 192 and width == 768 and args[2].shape[2] == CAP
        return (fused_step if fits else plain_step)(*args)

    return jax.shard_map(
        step, mesh=mesh, in_specs=placed, out_specs=(state,) * 4, check_vma=False
    )
```
